32 devices in a mesh: groups: 2 (over x), rows: 16 (over z, y, core).
Axes of the slice: x: 2, y: 2, z: 4, core: 2. Of those that a mesh axis runs over, the one named last changes fastest.
Arguments:
- features: bfloat16 [3, 256, 8192], P(None, ('groups', 'rows')), parts along dimension 1, may hold values from -6 to 6
- carried: bfloat16 [2, 256, 8192], P(None, ('groups', 'rows')), parts along dimension 1, may hold values from -6 to 6
- flow_shift: int32 [3, 32, 2], P(None, ('groups', 'rows')), parts along dimension 1, may hold values from -8 to 8, as said below
- clip_start: int32 [8], P('groups'), parts along dimension 0, may hold values from 0 to 3
- join_weight: bfloat16 [3, 576, 64], replicated, may hold values from -0.15625 to 0.15625
- res_weight: bfloat16 [4, 3, 192, 64], replicated, may hold values from -0.25 to 0.25
Outputs:
- propagated: bfloat16 [3, 256, 8192], P(None, ('groups', 'rows')), parts along dimension 1
The draws below stay inside these ranges and needn't reach their ends.
There are 2 independent parts, one for each index of `groups`. The reference program is written for one: setup_inputs(seed, part) draws one part's arguments, and reference() takes and returns one part's arrays. A program takes and returns all parts, laid end to end along the dimension named above; an argument that names none is the same for every part. Nothing has to cross between parts.
Inputs may be any that keep to these rules, and one draw needn't show every extreme that they name: `flow_shift`: both ends of the range occur in every draw. `clip_start`: 3 means that the owner begins no clip in these steps.
All inputs are finite; a program needn't handle non-finite values.
Results may differ from the reference program's by a relative error of at most 0.014.
Values may be sent and summed in bfloat16 or wider, within the bound.
A program may use at most 64 MiB of HBM per device.

```python
import jax
import jax.numpy as jnp
from jax import lax

C = 64
BAND = 8
WIN = 128
TICKS = 3
SECTIONS = 4
RES_BLOCKS = 2
MAXSHIFT = 8
SLOTS = 16
ALLROWS = 128
WIDE = 8192


def draw_flow_shift(key, part):
    total = TICKS * SLOTS * 2
    base = jax.random.randint(jax.random.fold_in(key, 11), (total,), -MAXSHIFT, MAXSHIFT + 1).astype(jnp.int32)
    spot_one = jax.random.randint(jax.random.fold_in(key, 12), (), 0, total)
    spot_gap = jax.random.randint(jax.random.fold_in(key, 13), (), 1, total)
    spot_two = (spot_one + spot_gap) % total
    base = base.at[spot_one].set(MAXSHIFT)
    base = base.at[spot_two].set(-MAXSHIFT)
    return base.reshape(TICKS, SLOTS, 2).astype(jnp.int32)


def touch_ends(entries, key, low, top_value):
    longest = entries.shape.index(max(entries.shape))
    spots = []
    for shift in (0, 1):
        where = [jax.random.randint(jax.random.fold_in(key, axis), (), 0, length) for axis, length in enumerate(entries.shape)]
        where[longest] = (where[longest] + shift) % entries.shape[longest]
        spots.append(tuple(where))
    return entries.at[spots[0]].set(low).at[spots[1]].set(top_value)


def level_of(rng, dims, pieces, low, top_value):
    def one(dim, shards_of):
        steps = jax.random.uniform(jax.random.fold_in(jax.random.fold_in(rng, 6), dim), (shards_of,), jnp.float32, low / len(pieces), top_value / len(pieces))
        return jnp.repeat(jnp.exp(steps), dims[dim] // shards_of).reshape((-1,) + (1,) * (len(dims) - dim - 1))

    loudness = one(*pieces[0])
    for cut in pieces[1:]:
        loudness = loudness * one(*cut)
    return loudness


def gaussian(own_key, shape, width, most, split=(), held_as=jnp.bfloat16):
    drawn = jax.random.normal(own_key, shape, jnp.float32) * width
    if len(split) > 0:
        drawn = level_of(own_key, shape, split, -0.22, 0.18) * drawn
    return jnp.clip(drawn, min=-most, max=most).astype(held_as)


def setup_inputs(seed: int = 0, part: int = 0) -> dict:
    splits = jax.random.split(jax.random.key(seed), 7)
    part_splits = jax.random.split(jax.random.fold_in(splits[6], part), 7)
    features = gaussian(part_splits[0], (TICKS, ALLROWS, WIDE), 1.0, 6.0, ((1, 16),))
    carried = gaussian(part_splits[1], (2, ALLROWS, WIDE), 1.0, 6.0, ((1, 16),))
    flow_shift = draw_flow_shift(jax.random.fold_in(jax.random.fold_in(splits[6], part), 71), part)
    clip_start = touch_ends(jax.random.randint(part_splits[3], (SECTIONS,), 0, TICKS + 1), jax.random.fold_in(part_splits[3], 1), 0, TICKS).astype(jnp.int32)
    join_weight = gaussian(splits[4], (3, 9 * C, C), (27 * C) ** -0.5, 0.15625)
    res_weight = gaussian(splits[5], (2 * RES_BLOCKS, 3, 3 * C, C), (9 * C) ** -0.5, 0.25)
    return {"features": features, "carried": carried, "flow_shift": flow_shift, "clip_start": clip_start, "join_weight": join_weight, "res_weight": res_weight}


def leaky_relu(values):
    return jnp.where(values >= 0, values, 0.1 * values)


def frame_conv(frames, weight):
    count = frames.shape[0]
    height = frames.shape[1]
    column_count = frames.shape[2]
    padded = jnp.pad(frames, ((0, 0), (1, 1), (1, 1), (0, 0)))
    columns = jnp.concatenate([padded[:, :, 0:column_count], padded[:, :, 1:column_count + 1], padded[:, :, 2:column_count + 2]], axis=3)
    depth_in = columns.shape[3]
    summed = jnp.dot(columns[:, 0:height].reshape(-1, depth_in), weight[0], preferred_element_type=jnp.float32)
    summed = summed + jnp.dot(columns[:, 1:height + 1].reshape(-1, depth_in), weight[1], preferred_element_type=jnp.float32)
    summed = summed + jnp.dot(columns[:, 2:height + 2].reshape(-1, depth_in), weight[2], preferred_element_type=jnp.float32)
    return summed.reshape(count, height, column_count, weight.shape[2])


def realign(latest, offsets):
    padded = jnp.pad(latest, ((0, 0), (0, 0), (MAXSHIFT * C, MAXSHIFT * C)))

    def pick(piece, offset):
        return lax.dynamic_slice_in_dim(piece, ((MAXSHIFT - offset) * C).astype(jnp.int32), WIN * C, 1)

    return jax.vmap(pick)(padded, offsets.astype(jnp.int32))


def reference(features, carried, flow_shift, clip_start, join_weight, res_weight):
    slots = flow_shift.shape[1]
    per_owner = slots // SECTIONS
    offset_lead = per_owner // 2
    latest = jnp.roll(carried[0].reshape(slots, BAND, WIN * C), -offset_lead, axis=0)
    earlier = jnp.roll(carried[1].reshape(slots, BAND, WIN * C), -offset_lead, axis=0)
    shifts_all = jnp.roll(flow_shift, -offset_lead, axis=1)
    owner_of = (jnp.arange(slots) // per_owner).astype(jnp.int32)
    start_slot = clip_start[owner_of]
    results = []
    for frame_tick in range(TICKS):
        keep_state = (start_slot != frame_tick)[:, None, None]
        latest = jnp.where(keep_state, latest, jnp.zeros_like(latest))
        earlier = jnp.where(keep_state, earlier, jnp.zeros_like(earlier))
        warped_one = realign(latest, shifts_all[frame_tick, :, 0])
        warped_two = realign(earlier, shifts_all[frame_tick, :, 1])
        frame_feat = jnp.roll(features[frame_tick].reshape(slots, BAND, WIN * C), -offset_lead, axis=0)
        stacked = jnp.concatenate([warped_one.reshape(slots, BAND, WIN, C), warped_two.reshape(slots, BAND, WIN, C), frame_feat.reshape(slots, BAND, WIN, C)], axis=3)
        frames = stacked.reshape(SECTIONS, per_owner * BAND, WIN, 3 * C)
        current = leaky_relu(frame_conv(frames, join_weight)).astype(jnp.bfloat16)
        for res_index in range(RES_BLOCKS):
            middle = jnp.maximum(frame_conv(current, res_weight[2 * res_index]), 0.0).astype(jnp.bfloat16)
            current = (current.astype(jnp.float32) + frame_conv(middle, res_weight[2 * res_index + 1])).astype(jnp.bfloat16)
        flattened = current.reshape(slots, BAND, WIN * C)
        results.append(jnp.roll(flattened, offset_lead, axis=0).reshape(slots * BAND, WIN * C))
        latest, earlier = jnp.roll(flattened, per_owner, axis=0), jnp.roll(latest, per_owner, axis=0)
    return jnp.stack(results)
```

```python
import functools

import jax
import jax.numpy as jnp
from jax import lax
from jax.experimental import pallas as pl
from jax.experimental.pallas import tpu as pltpu
from jax.sharding import PartitionSpec as P

SECTIONS = 4
MAXSHIFT = 8
LANES = 128
LEAD = 4


def band_blocks(taps):
    zero = jnp.zeros_like(taps[0])
    blank = jnp.concatenate([zero, zero], axis=1)
    first = jnp.concatenate([taps[0], zero], axis=1)
    second = jnp.concatenate([taps[1], taps[0]], axis=1)
    third = jnp.concatenate([taps[2], taps[1]], axis=1)
    fourth = jnp.concatenate([zero, taps[2]], axis=1)
    return [
        (second, blank),
        (third, first),
        (fourth, second),
        (blank, third),
        (blank, fourth),
        (first, blank),
    ]


def warp(state, shift):
    pairs, rows, lanes = state.shape
    pad = MAXSHIFT // 2
    amount = MAXSHIFT - shift
    moved = jnp.concatenate(
        [
            jnp.zeros((pad, rows, lanes), state.dtype),
            state,
            jnp.zeros((3 * pad, rows, lanes), state.dtype),
        ],
        axis=0,
    )
    step = MAXSHIFT
    while step >= 1:
        bit = (lax.div(amount, 2 * step) % 2 == 1)[None]
        moved = jnp.where(bit, moved[step : moved.shape[0]], moved[: moved.shape[0] - step])
        step //= 2
    moved = moved[: pairs + 1]
    swapped = pltpu.roll(moved, lanes // 2, axis=2)
    low = lax.broadcasted_iota(jnp.int32, (1, rows, lanes), 2) < lanes // 2
    odd = (amount % 2 == 1)[None]
    return jnp.where(odd, jnp.where(low, swapped[:pairs], swapped[1:]), moved[:pairs])


def fill_columns(left_ref, low, high, first):
    groups, rows, lanes = low.shape
    gap = jnp.zeros((1, rows, lanes), low.dtype)
    after = jnp.concatenate([low[1:], gap], axis=0)
    before = jnp.concatenate([gap, high[:-1]], axis=0)
    left_half = lax.broadcasted_iota(jnp.int32, (1, rows, lanes), 2) < lanes // 2
    edge = jnp.where(left_half, after, before)
    window = 16
    for kernel_row in range(3):
        back = (first + kernel_row) % rows
        for part, values in enumerate((low, high, edge)):
            turned = values if back == 0 else pltpu.roll(values, rows - back, axis=1)
            column = (3 * kernel_row + part) * lanes
            left_ref[:, column : column + lanes] = (
                turned[:, :window].reshape(groups * window, lanes).astype(jnp.bfloat16)
            )


def kernel(
    ticks, blocks, row_count, feat, carried, flow, clip, join_w, res_w, out,
    band_w, left, total, sent, above, below, brought, shift_out, shift_in, made, deliver,
    halo_send, halo_recv, feat_send, feat_recv, flow_send, flow_recv, out_send, out_recv, local_sem,
):
    pairs, band_rows = feat.shape[1], feat.shape[2]
    groups = pairs // 2
    channels = join_w.shape[2]
    band_count = row_count // SECTIONS
    me = lax.axis_index("rows")
    spot = lax.rem(me - band_count // 2 + row_count, row_count)
    band = lax.rem(spot, band_count)
    owner = lax.div(spot, band_count)

    def at(offset):
        return {"rows": lax.rem(me + offset % row_count, row_count)}

    offsets = {1, row_count - 1}
    for tick in range(1, ticks):
        offsets |= {(band_count * tick) % row_count, (-band_count * tick) % row_count}
    barrier = pltpu.get_barrier_semaphore()
    for offset in sorted(offsets):
        pl.semaphore_signal(
            barrier, inc=1, device_id=at(offset), device_id_type=pl.DeviceIdType.MESH
        )
    for tick in range(1, ticks):
        for which in range(2):
            shift_out[tick, which] = jnp.full((8, LANES), flow[tick, 0, which], jnp.int32)
    pl.semaphore_wait(barrier, len(offsets))

    pending = []

    def send(source, target, send_sem, recv_sem, offset):
        copy = pltpu.make_async_remote_copy(
            src_ref=source, dst_ref=target, send_sem=send_sem, recv_sem=recv_sem,
            device_id=at(offset), device_id_type=pl.DeviceIdType.MESH,
        )
        copy.start()
        pending.append(copy)
        return copy

    halos = {}

    def send_halo(tick, slot, source):
        halos[tick, slot] = (
            send(source, above.at[tick, slot], halo_send.at[tick, slot, 0],
                 halo_recv.at[tick, slot, 0], 1),
            send(source, below.at[tick, slot], halo_send.at[tick, slot, 1],
                 halo_recv.at[tick, slot, 1], -1),
        )

    def keep(tick):
        begins = clip[lax.rem(owner + tick, SECTIONS)]
        return (jnp.full((8, LANES), begins, jnp.int32) != tick)[None]

    def reset(state, tick):
        return jnp.where(keep(tick), state, 0.0)

    send_halo(0, 2, feat.at[0])
    latest = reset(carried[0].astype(jnp.float32), 0)
    earlier = reset(carried[1].astype(jnp.float32), 0)
    for slot, state in ((1, earlier), (0, latest)):
        shift = jnp.full((8, LANES), flow[0, 0, slot], jnp.int32)
        sent[0, slot] = warp(state, shift).astype(jnp.bfloat16)
        send_halo(0, slot, sent.at[0, slot])
    feats, flows = {}, {}
    for tick in range(1, ticks):
        flows[tick] = send(shift_out.at[tick], shift_in.at[tick], flow_send.at[tick],
                           flow_recv.at[tick], -band_count * tick)
        feats[tick] = send(feat.at[tick], brought.at[tick], feat_send.at[tick],
                           feat_recv.at[tick], -band_count * tick)
    made[0] = latest.astype(jnp.bfloat16)

    for layer in range(3 + 2 * blocks):
        for kernel_row in range(3):
            taps = []
            for column in range(3):
                if layer < 3:
                    start = (column * 3 + layer) * channels
                    taps.append(join_w[kernel_row, start : start + channels, :])
                else:
                    start = column * channels
                    taps.append(res_w[layer - 3, kernel_row, start : start + channels, :])
            for index, (left_part, right_part) in enumerate(band_blocks(taps)):
                start = (kernel_row * 6 + index) * channels
                band_w[layer, start : start + channels, 0:LANES] = left_part
                band_w[layer, start : start + channels, LANES : 2 * LANES] = right_part

    def matmul(layer):
        return jnp.dot(left[...], band_w[layer], preferred_element_type=jnp.float32)

    window = 16
    line = lax.broadcasted_iota(jnp.int32, (1, window, 2 * LANES), 1)
    inside = ((line >= LEAD) | (band > 0)) & (
        (line < LEAD + band_rows) | (band < band_count - 1)
    )

    def settle(values):
        rounded = values.reshape(groups, window, 2 * LANES).astype(jnp.bfloat16)
        return jnp.where(inside, rounded.astype(jnp.float32), 0.0)

    def join(tick, slot, own):
        for copy in halos[tick, slot]:
            copy.wait_recv()
        upper = above[tick, slot].astype(jnp.float32)
        lower = below[tick, slot].astype(jnp.float32)
        upper = jnp.where(band > 0, upper, 0.0)
        lower = jnp.where(band < band_count - 1, lower, 0.0)
        tall = jnp.concatenate([upper, own.astype(jnp.float32), lower], axis=1)
        tall = tall.reshape(groups, 2, 3 * band_rows, LANES)
        fill_columns(left, tall[:, 0], tall[:, 1], band_rows - LEAD - 1)
        return matmul(slot)

    for tick in range(ticks):
        own_feat = feat[0] if tick == 0 else brought[tick]
        total[...] = join(tick, 2, own_feat)
        total[...] += join(tick, 1, sent[tick, 1])
        summed = total[...] + join(tick, 0, sent[tick, 0])
        current = settle(jnp.where(summed >= 0, summed, 0.1 * summed))
        total[...] = current.reshape(groups * window, 2 * LANES)

        if tick + 1 < ticks:
            feats[tick + 1].wait_recv()
            send_halo(tick + 1, 2, brought.at[tick + 1])
            flows[tick + 1].wait_recv()
            earlier = reset(made[tick].astype(jnp.float32), tick + 1)
            sent[tick + 1, 1] = warp(earlier, shift_in[tick + 1, 1]).astype(jnp.bfloat16)
            send_halo(tick + 1, 1, sent.at[tick + 1, 1])

        for block in range(blocks):
            fill_columns(left, current[..., :LANES], current[..., LANES:], window - 1)
            middle = settle(jnp.maximum(matmul(3 + 2 * block), 0.0))
            fill_columns(left, middle[..., :LANES], middle[..., LANES:], window - 1)
            current = settle(total[...] + matmul(4 + 2 * block))
            total[...] = current.reshape(groups * window, 2 * LANES)

        done = pltpu.roll(current, window - LEAD, axis=1)[:, :band_rows]
        state = jnp.stack([done[..., :LANES], done[..., LANES:]], axis=1)
        state = state.reshape(pairs, band_rows, LANES)
        deliver[tick] = state.astype(jnp.bfloat16)
        if tick + 1 < ticks:
            latest = reset(state, tick + 1)
            made[tick + 1] = latest.astype(jnp.bfloat16)
            sent[tick + 1, 0] = warp(latest, shift_in[tick + 1, 0]).astype(jnp.bfloat16)
            send_halo(tick + 1, 0, sent.at[tick + 1, 0])
        if tick == 0:
            home = pltpu.make_async_copy(deliver.at[0], out.at[0], local_sem)
            home.start()
        else:
            halos["out", tick] = (
                send(deliver.at[tick], out.at[tick], out_send.at[tick], out_recv.at[tick],
                     band_count * tick),
            )

    home.wait()
    for copy in pending:
        copy.wait_send()
    for tick in range(1, ticks):
        halos["out", tick][0].wait_recv()


def shards(features, carried, flow_shift, clip_start, join_weight, res_weight):
    ticks, band_rows, wide = features.shape
    channels = join_weight.shape[2]
    blocks = res_weight.shape[0] // 2
    row_count = lax.axis_size("rows")
    pairs = wide // LANES
    groups = pairs // 2

    def paired(array):
        return array.reshape(-1, band_rows, pairs, LANES).transpose(0, 2, 1, 3)

    def vmem(*shape):
        return pltpu.VMEM(shape, jnp.bfloat16)

    whole = pl.BlockSpec(memory_space=pltpu.VMEM)
    scalars = pl.BlockSpec(memory_space=pltpu.SMEM)
    state = (pairs, band_rows, LANES)
    dma = pltpu.SemaphoreType.DMA
    layers = 3 + 2 * blocks
    result = pl.pallas_call(
        functools.partial(kernel, ticks, blocks, row_count),
        out_shape=jax.ShapeDtypeStruct((ticks, *state), jnp.bfloat16),
        in_specs=[whole, whole, scalars, scalars, whole, whole],
        out_specs=pl.BlockSpec(memory_space=pl.ANY),
        scratch_shapes=[
            vmem(layers, 18 * channels, 2 * LANES),
            vmem(groups * 16, 9 * LANES),
            pltpu.VMEM((groups * 16, 2 * LANES), jnp.float32),
            vmem(ticks, 2, *state),
            vmem(ticks, 3, *state),
            vmem(ticks, 3, *state),
            vmem(ticks, *state),
            pltpu.VMEM((ticks, 2, 8, LANES), jnp.int32),
            pltpu.VMEM((ticks, 2, 8, LANES), jnp.int32),
            vmem(ticks, *state),
            vmem(ticks, *state),
            dma((ticks, 3, 2)),
            dma((ticks, 3, 2)),
            dma((ticks,)),
            dma((ticks,)),
            dma((ticks,)),
            dma((ticks,)),
            dma((ticks,)),
            dma((ticks,)),
            dma,
        ],
        compiler_params=pltpu.CompilerParams(
            collective_id=0, has_side_effects=True, vmem_limit_bytes=48 * 1024 * 1024
        ),
    )(paired(features), paired(carried), flow_shift, clip_start, join_weight, res_weight)
    return result.transpose(0, 2, 1, 3).reshape(ticks, band_rows, wide)


def solution(mesh):
    in_specs = (
        P(None, ("groups", "rows"), None),
        P(None, ("groups", "rows"), None),
        P(None, ("groups", "rows"), None),
        P("groups"),
        P(),
        P(),
    )
    out_specs = P(None, ("groups", "rows"), None)
    return jax.shard_map(shards, mesh=mesh, in_specs=in_specs, out_specs=out_specs, check_vma=False)
```

```python
import functools

import jax
import jax.numpy as jnp
from jax import lax
from jax.experimental import pallas as pl
from jax.experimental.pallas import tpu as pltpu
from jax.sharding import PartitionSpec as P

SECTIONS = 4
MAXSHIFT = 8
LANES = 128


def band_blocks(taps):
    zero = jnp.zeros_like(taps[0])
    blank = jnp.concatenate([zero, zero], axis=1)
    first = jnp.concatenate([taps[0], zero], axis=1)
    second = jnp.concatenate([taps[1], taps[0]], axis=1)
    third = jnp.concatenate([taps[2], taps[1]], axis=1)
    fourth = jnp.concatenate([zero, taps[2]], axis=1)
    return [
        (second, blank),
        (third, first),
        (fourth, second),
        (blank, third),
        (blank, fourth),
        (first, blank),
    ]


def turn(values, step):
    return pltpu.roll(values, step % values.shape[1], axis=1)


def warp(state, shift):
    groups = state.shape[1]
    low, high = state[..., :LANES], state[..., LANES:]
    lane = lax.broadcasted_iota(jnp.int32, (1, groups, LANES), 2)
    group = lax.broadcasted_iota(jnp.int32, (1, groups, LANES), 1)
    left_half = lane < LANES // 2
    shift = shift[None]
    quads = lax.shift_right_arithmetic(shift, 2)
    for mask, step in ((quads < 0, -4), ((quads & 2) != 0, 2), ((quads & 1) != 0, 1)):
        low = jnp.where(mask, turn(low, step), low)
        high = jnp.where(mask, turn(high, step), high)
    two = (shift & 2) != 0
    low, high = jnp.where(two, turn(high, 1), low), jnp.where(two, low, high)
    one = (shift & 1) != 0
    low_swap = pltpu.roll(low, LANES // 2, axis=2)
    high_swap = pltpu.roll(high, LANES // 2, axis=2)
    low = jnp.where(one, jnp.where(left_half, turn(high_swap, 1), low_swap), low)
    high = jnp.where(one, jnp.where(left_half, low_swap, high_swap), high)
    origin = group * 4 + lane // (LANES // 2) - shift
    low = jnp.where((origin >= 0) & (origin < 4 * groups), low, 0.0)
    high = jnp.where((origin >= -2) & (origin < 4 * groups - 2), high, 0.0)
    return jnp.concatenate([low, high], axis=-1).astype(jnp.bfloat16)


def edges(values):
    groups = values.shape[1]
    group = lax.broadcasted_iota(jnp.int32, (1, groups, LANES), 1)
    lane = lax.broadcasted_iota(jnp.int32, (1, groups, LANES), 2)
    left_half = lane < LANES // 2
    edge = jnp.where(left_half, turn(values[..., :LANES], -1), turn(values[..., LANES:], 1))
    outside = (left_half & (group == groups - 1)) | ((lane >= LANES // 2) & (group == 0))
    return jnp.where(outside, 0.0, edge).astype(jnp.bfloat16)


def taps_of(main, edge, rows):
    parts = [main[a : a + rows] for a in range(3)] + [edge[a : a + rows] for a in range(3)]
    return jnp.concatenate(parts, axis=-1).reshape(rows * main.shape[1], 9 * LANES)


def kernel(
    ticks, blocks, row_count, feat, carried, flow, clip, join_w, res_w, out,
    band_w, grown, grown_edge, current, current_edge, middle, middle_edge, total, made,
    deliver, shift_out, shift_in,
    halo_send, halo_recv, feat_send, feat_recv, flow_send, flow_recv, out_send, out_recv, local_sem,
):
    band_rows, groups, wide = feat.shape[1:]
    channels = join_w.shape[2]
    rim = 1 + 2 * blocks
    own = pl.ds(rim, band_rows)
    band_count = row_count // SECTIONS
    me = lax.axis_index("rows")
    spot = lax.rem(me - band_count // 2 + row_count, row_count)
    band = lax.rem(spot, band_count)
    owner = lax.div(spot, band_count)

    def at(offset):
        return {"rows": lax.rem(me + offset % row_count, row_count)}

    offsets = {1, row_count - 1}
    for tick in range(1, ticks):
        offsets |= {(band_count * tick) % row_count, (-band_count * tick) % row_count}
    barrier = pltpu.get_barrier_semaphore()
    for offset in sorted(offsets):
        pl.semaphore_signal(
            barrier, inc=1, device_id=at(offset), device_id_type=pl.DeviceIdType.MESH
        )

    pending = []

    def send(source, target, send_sem, recv_sem, offset):
        copy = pltpu.make_async_remote_copy(
            src_ref=source, dst_ref=target, send_sem=send_sem, recv_sem=recv_sem,
            device_id=at(offset), device_id_type=pl.DeviceIdType.MESH,
        )
        copy.start()
        pending.append(copy)
        return copy

    halos = {}

    def send_halo(tick, slot):
        block = grown.at[tick, slot]
        halos[tick, slot] = (
            send(block.at[pl.ds(band_rows, rim)], block.at[pl.ds(0, rim)],
                 halo_send.at[tick, slot, 0], halo_recv.at[tick, slot, 0], 1),
            send(block.at[pl.ds(rim, rim)], block.at[pl.ds(rim + band_rows, rim)],
                 halo_send.at[tick, slot, 1], halo_recv.at[tick, slot, 1], -1),
        )

    def reset(state, tick):
        begins = clip[lax.rem(owner + tick, SECTIONS)]
        keep = jnp.full((groups, wide), begins, jnp.int32) != tick
        return jnp.where(keep[None], state, 0.0)

    grown[0, 2, own] = feat[0]
    for tick in range(1, ticks):
        for which in range(2):
            shift_out[tick, which] = jnp.full((groups, LANES), flow[tick, 0, which], jnp.int32)
    pl.semaphore_wait(barrier, len(offsets))
    send_halo(0, 2)
    for slot in (1, 0):
        state = reset(carried[slot].astype(jnp.float32), 0)
        if slot == 0:
            made[0] = state.astype(jnp.bfloat16)
        shift = jnp.full((groups, LANES), flow[0, 0, slot], jnp.int32)
        grown[0, slot, own] = warp(state, shift)
        send_halo(0, slot)
    feats, flows = {}, {}
    for tick in range(1, ticks):
        flows[tick] = send(shift_out.at[tick], shift_in.at[tick], flow_send.at[tick],
                           flow_recv.at[tick], -band_count * tick)

    def fetch(tick):
        feats[tick] = send(feat.at[tick], grown.at[tick, 2, own], feat_send.at[tick],
                           feat_recv.at[tick], -band_count * tick)

    for layer in range(3 + 2 * blocks):
        for kernel_row in range(3):
            taps = []
            for column in range(3):
                if layer < 3:
                    start = (column * 3 + layer) * channels
                    taps.append(join_w[kernel_row, start : start + channels, :])
                else:
                    start = column * channels
                    taps.append(res_w[layer - 3, kernel_row, start : start + channels, :])
            for index, (left_part, right_part) in enumerate(band_blocks(taps)):
                if index < 4:
                    start = (kernel_row * 4 + index) * channels
                else:
                    start = (12 + kernel_row * 2 + index - 4) * channels
                band_w[layer, start : start + channels, 0:LANES] = left_part
                band_w[layer, start : start + channels, LANES : 2 * LANES] = right_part

    def matmul(main, edge, rows, layer):
        return jnp.dot(
            taps_of(main, edge, rows), band_w[layer], preferred_element_type=jnp.float32
        )

    def clear(refs, rows, margin):
        @pl.when(band == 0)
        def _():
            for ref in refs:
                ref[0:margin] = jnp.zeros((margin, *ref.shape[1:]), ref.dtype)

        @pl.when(band == band_count - 1)
        def _():
            for ref in refs:
                ref[rows - margin : rows] = jnp.zeros((margin, *ref.shape[1:]), ref.dtype)

    def settle(main, edge, values, rows):
        rounded = values.reshape(rows, groups, wide).astype(jnp.bfloat16)
        main[0:rows] = rounded
        edge[0:rows] = edges(rounded.astype(jnp.float32))
        clear((main, edge), rows, (rows - band_rows) // 2)

    most = band_rows + 2 * rim - 2

    def join(tick, slot):
        for copy in halos[tick, slot]:
            copy.wait_recv()
        block = grown.at[tick, slot]
        clear((block,), band_rows + 2 * rim, rim)
        grown_edge[slot] = edges(block[...].astype(jnp.float32))
        return matmul(block, grown_edge.at[slot], most, slot)

    for tick in range(ticks):
        total[...] = join(tick, 2)
        total[...] += join(tick, 1)
        summed = total[...] + join(tick, 0)
        if tick == 0 and ticks > 1:
            fetch(1)
        settle(current, current_edge, jnp.where(summed >= 0, summed, 0.1 * summed), most)
        rows = most
        for block in range(blocks):
            rows -= 2
            hidden = jnp.maximum(matmul(current, current_edge, rows, 3 + 2 * block), 0.0)
            settle(middle, middle_edge, hidden, rows)
            if block == 0 and tick + 1 < ticks:
                flows[tick + 1].wait_recv()
                earlier = reset(made[tick].astype(jnp.float32), tick + 1)
                grown[tick + 1, 1, own] = warp(earlier, shift_in[tick + 1, 1])
                send_halo(tick + 1, 1)
                feats[tick + 1].wait_recv()
                send_halo(tick + 1, 2)
                if tick + 2 < ticks:
                    fetch(tick + 2)
            rows -= 2
            kept = current[2 : 2 + rows].astype(jnp.float32).reshape(rows * groups, wide)
            added = kept + matmul(middle, middle_edge, rows, 4 + 2 * block)
            if block + 1 < blocks:
                settle(current, current_edge, added, rows)
        state = added.reshape(band_rows, groups, wide).astype(jnp.bfloat16)
        deliver[tick] = state
        if tick == 0:
            home = pltpu.make_async_copy(deliver.at[0], out.at[0], local_sem)
            home.start()
        if tick + 1 < ticks:
            latest = reset(state.astype(jnp.float32), tick + 1)
            made[tick + 1] = latest.astype(jnp.bfloat16)
            grown[tick + 1, 0, own] = warp(latest, shift_in[tick + 1, 0])
            send_halo(tick + 1, 0)
        if tick > 0:
            halos["out", tick] = (
                send(deliver.at[tick], out.at[tick], out_send.at[tick], out_recv.at[tick],
                     band_count * tick),
            )

    home.wait()
    for copy in pending:
        copy.wait_send()
    for tick in range(1, ticks):
        halos["out", tick][0].wait_recv()


def shards(features, carried, flow_shift, clip_start, join_weight, res_weight):
    ticks, band_rows, line = features.shape
    channels = join_weight.shape[2]
    blocks = res_weight.shape[0] // 2
    row_count = lax.axis_size("rows")
    wide = 2 * LANES
    groups = line // wide
    rim = 1 + 2 * blocks
    most = band_rows + 2 * rim - 2

    def grouped(array):
        return array.reshape(-1, band_rows, groups, wide)

    def vmem(*shape):
        return pltpu.VMEM(shape, jnp.bfloat16)

    whole = pl.BlockSpec(memory_space=pltpu.VMEM)
    scalars = pl.BlockSpec(memory_space=pltpu.SMEM)
    state = (band_rows, groups, wide)
    dma = pltpu.SemaphoreType.DMA
    result = pl.pallas_call(
        functools.partial(kernel, ticks, blocks, row_count),
        out_shape=jax.ShapeDtypeStruct((ticks, *state), jnp.bfloat16),
        in_specs=[whole, whole, scalars, scalars, whole, whole],
        out_specs=pl.BlockSpec(memory_space=pl.ANY),
        scratch_shapes=[
            vmem(3 + 2 * blocks, 18 * channels, wide),
            vmem(ticks, 3, band_rows + 2 * rim, groups, wide),
            vmem(3, band_rows + 2 * rim, groups, LANES),
            vmem(most, groups, wide),
            vmem(most, groups, LANES),
            vmem(most, groups, wide),
            vmem(most, groups, LANES),
            pltpu.VMEM((most * groups, wide), jnp.float32),
            vmem(ticks, *state),
            vmem(ticks, *state),
            pltpu.VMEM((ticks, 2, groups, LANES), jnp.int32),
            pltpu.VMEM((ticks, 2, groups, LANES), jnp.int32),
            dma((ticks, 3, 2)),
            dma((ticks, 3, 2)),
            dma((ticks,)),
            dma((ticks,)),
            dma((ticks,)),
            dma((ticks,)),
            dma((ticks,)),
            dma((ticks,)),
            dma,
        ],
        compiler_params=pltpu.CompilerParams(
            collective_id=0, has_side_effects=True, vmem_limit_bytes=48 * 1024 * 1024
        ),
    )(grouped(features), grouped(carried), flow_shift, clip_start, join_weight, res_weight)
    return result.reshape(ticks, band_rows, line)


def solution(mesh):
    in_specs = (
        P(None, ("groups", "rows"), None),
        P(None, ("groups", "rows"), None),
        P(None, ("groups", "rows"), None),
        P("groups"),
        P(),
        P(),
    )
    out_specs = P(None, ("groups", "rows"), None)
    return jax.shard_map(shards, mesh=mesh, in_specs=in_specs, out_specs=out_specs, check_vma=False)
```

```python
import functools

import jax
import jax.numpy as jnp
from jax import lax
from jax.experimental import pallas as pl
from jax.experimental.pallas import tpu as pltpu
from jax.sharding import PartitionSpec as P

SECTIONS = 4
MAXSHIFT = 8
LANES = 128


def band_blocks(taps):
    zero = jnp.zeros_like(taps[0])
    blank = jnp.concatenate([zero, zero], axis=1)
    first = jnp.concatenate([taps[0], zero], axis=1)
    second = jnp.concatenate([taps[1], taps[0]], axis=1)
    third = jnp.concatenate([taps[2], taps[1]], axis=1)
    fourth = jnp.concatenate([zero, taps[2]], axis=1)
    return [
        (second, blank),
        (third, first),
        (fourth, second),
        (blank, third),
        (blank, fourth),
        (first, blank),
    ]


def turn(values, step):
    return pltpu.roll(values, step % values.shape[1], axis=1)


def warp(state, shift):
    groups = state.shape[1]
    low, high = state[..., :LANES], state[..., LANES:]
    lane = lax.broadcasted_iota(jnp.int32, (1, groups, LANES), 2)
    group = lax.broadcasted_iota(jnp.int32, (1, groups, LANES), 1)
    left_half = lane < LANES // 2
    shift = shift[None]
    quads = lax.shift_right_arithmetic(shift, 2)
    for mask, step in ((quads < 0, -4), ((quads & 2) != 0, 2), ((quads & 1) != 0, 1)):
        low = jnp.where(mask, turn(low, step), low)
        high = jnp.where(mask, turn(high, step), high)
    two = (shift & 2) != 0
    low, high = jnp.where(two, turn(high, 1), low), jnp.where(two, low, high)
    one = (shift & 1) != 0
    low_swap = pltpu.roll(low, LANES // 2, axis=2)
    high_swap = pltpu.roll(high, LANES // 2, axis=2)
    low = jnp.where(one, jnp.where(left_half, turn(high_swap, 1), low_swap), low)
    high = jnp.where(one, jnp.where(left_half, low_swap, high_swap), high)
    origin = group * 4 + lane // (LANES // 2) - shift
    low = jnp.where((origin >= 0) & (origin < 4 * groups), low, 0.0)
    high = jnp.where((origin >= -2) & (origin < 4 * groups - 2), high, 0.0)
    return jnp.concatenate([low, high], axis=-1).astype(jnp.bfloat16)


def edges(values):
    groups = values.shape[1]
    group = lax.broadcasted_iota(jnp.int32, (1, groups, LANES), 1)
    lane = lax.broadcasted_iota(jnp.int32, (1, groups, LANES), 2)
    left_half = lane < LANES // 2
    edge = jnp.where(left_half, turn(values[..., :LANES], -1), turn(values[..., LANES:], 1))
    outside = (left_half & (group == groups - 1)) | ((lane >= LANES // 2) & (group == 0))
    return jnp.where(outside, 0.0, edge).astype(jnp.bfloat16)


def taps_of(main, edge, rows):
    parts = [main[a : a + rows] for a in range(3)] + [edge[a : a + rows] for a in range(3)]
    return jnp.concatenate(parts, axis=-1).reshape(rows * main.shape[1], 9 * LANES)


def kernel(
    ticks, blocks, row_count, feat, carried, flow, clip, join_w, res_w, out,
    band_w, grown, grown_edge, current, current_edge, middle, middle_edge, total, made,
    deliver, shift_out, shift_in,
    halo_send, halo_recv, feat_send, feat_recv, flow_send, flow_recv, out_send, out_recv, local_sem,
):
    band_rows, groups, wide = feat.shape[1:]
    channels = join_w.shape[2]
    rim = 1 + 2 * blocks
    own = pl.ds(rim, band_rows)
    band_count = row_count // SECTIONS
    me = lax.axis_index("rows")
    spot = lax.rem(me - band_count // 2 + row_count, row_count)
    band = lax.rem(spot, band_count)
    owner = lax.div(spot, band_count)

    def at(offset):
        return {"rows": lax.rem(me + offset, row_count)}

    offsets = {1, row_count - 1}
    for tick in range(1, ticks):
        offsets |= {(band_count * tick) % row_count, (-band_count * tick) % row_count}
    barrier = pltpu.get_barrier_semaphore()
    for offset in sorted(offsets):
        pl.semaphore_signal(
            barrier, inc=1, device_id=at(offset), device_id_type=pl.DeviceIdType.MESH
        )

    def copy_of(source, target, send_sem, recv_sem, offset):
        return pltpu.make_async_remote_copy(
            src_ref=source, dst_ref=target, send_sem=send_sem, recv_sem=recv_sem,
            device_id=at(offset), device_id_type=pl.DeviceIdType.MESH,
        )

    def halo(tick, slot):
        block = grown.at[tick, slot]
        return (
            copy_of(block.at[pl.ds(band_rows, rim)], block.at[pl.ds(0, rim)],
                    halo_send.at[tick, slot, 0], halo_recv.at[tick, slot, 0], 1),
            copy_of(block.at[pl.ds(rim, rim)], block.at[pl.ds(rim + band_rows, rim)],
                    halo_send.at[tick, slot, 1], halo_recv.at[tick, slot, 1], row_count - 1),
        )

    def send_halo(tick, slot):
        for copy in halo(tick, slot):
            copy.start()

    def backwards(tick):
        return row_count - band_count * tick

    def fetched(tick):
        return copy_of(feat.at[tick], grown.at[tick, 2, own], feat_send.at[tick],
                       feat_recv.at[tick], backwards(tick))

    def shifts(tick):
        return copy_of(shift_out.at[tick], shift_in.at[tick], flow_send.at[tick],
                       flow_recv.at[tick], backwards(tick))

    def delivered(tick):
        return copy_of(deliver.at[tick], out.at[tick], out_send.at[tick], out_recv.at[tick],
                       band_count * tick)

    home = pltpu.make_async_copy(deliver.at[0], out.at[0], local_sem)

    def reset(state, tick):
        begins = clip[lax.rem(owner + tick, SECTIONS)]
        keep = jnp.full((groups, wide), begins, jnp.int32) != tick
        return jnp.where(keep[None], state, 0.0)

    grown[0, 2, own] = feat[0]
    for tick in range(1, ticks):
        for which in range(2):
            shift_out[tick, which] = jnp.full((groups, LANES), flow[0, which, tick], jnp.int32)
    pl.semaphore_wait(barrier, len(offsets))
    send_halo(0, 2)
    for slot in (1, 0):
        state = reset(carried[slot].astype(jnp.float32), 0)
        if slot == 0:
            made[0] = state.astype(jnp.bfloat16)
        shift = jnp.full((groups, LANES), flow[0, slot, 0], jnp.int32)
        grown[0, slot, own] = warp(state, shift)
        send_halo(0, slot)
    for tick in range(1, ticks):
        shifts(tick).start()

    depth = 18 * channels
    for layer in range(3 + 2 * blocks):
        base = layer * depth
        for kernel_row in range(3):
            taps = []
            for column in range(3):
                if layer < 3:
                    start = (column * 3 + layer) * channels
                    taps.append(join_w[kernel_row, start : start + channels, :])
                else:
                    start = column * channels
                    taps.append(res_w[layer - 3, kernel_row, start : start + channels, :])
            for index, (left_part, right_part) in enumerate(band_blocks(taps)):
                if index < 4:
                    start = (kernel_row * 4 + index) * channels
                else:
                    start = (12 + kernel_row * 2 + index - 4) * channels
                band_w[base + start : base + start + channels, 0:LANES] = left_part
                band_w[base + start : base + start + channels, LANES : 2 * LANES] = right_part

    if ticks > 1:
        fetched(1).start()

    def matmul(left, layer, count=1):
        right = band_w[layer * depth : (layer + count) * depth]
        return jnp.dot(left, right, preferred_element_type=jnp.float32)

    def clear(refs, rows, margin):
        @pl.when(band == 0)
        def _():
            for ref in refs:
                ref[0:margin] = jnp.zeros((margin, *ref.shape[1:]), ref.dtype)

        @pl.when(band == band_count - 1)
        def _():
            for ref in refs:
                ref[rows - margin : rows] = jnp.zeros((margin, *ref.shape[1:]), ref.dtype)

    def settle(main, edge, values, rows):
        rounded = values.reshape(rows, groups, wide).astype(jnp.bfloat16)
        main[0:rows] = rounded
        edge[0:rows] = edges(rounded.astype(jnp.float32))
        clear((main, edge), rows, (rows - band_rows) // 2)

    most = band_rows + 2 * rim - 2

    def join_taps(tick, slot):
        for copy in halo(tick, slot):
            copy.wait_recv()
        block = grown.at[tick, slot]
        clear((block,), band_rows + 2 * rim, rim)
        grown_edge[slot] = edges(block[...].astype(jnp.float32))
        return taps_of(block, grown_edge.at[slot], most)

    def one_tick(tick, nothing):
        side = jnp.concatenate([join_taps(tick, 1), join_taps(tick, 2)], axis=-1)
        total[...] = matmul(side, 1, 2)
        summed = total[...] + matmul(join_taps(tick, 0), 0)
        settle(current, current_edge, jnp.where(summed >= 0, summed, 0.1 * summed), most)
        rows = most
        for block in range(blocks):
            rows -= 2
            hidden = matmul(taps_of(current, current_edge, rows), 3 + 2 * block)
            settle(middle, middle_edge, jnp.maximum(hidden, 0.0), rows)
            if block == 0:
                @pl.when(tick + 1 < ticks)
                def _():
                    shifts(tick + 1).wait_recv()
                    earlier = reset(made[tick].astype(jnp.float32), tick + 1)
                    grown[tick + 1, 1, own] = warp(earlier, shift_in[tick + 1, 1])
                    send_halo(tick + 1, 1)
            if block == blocks - 1:
                @pl.when(tick + 1 < ticks)
                def _():
                    fetched(tick + 1).wait_recv()
                    send_halo(tick + 1, 2)

                @pl.when(tick + 2 < ticks)
                def _():
                    fetched(tick + 2).start()
            rows -= 2
            kept = current[2 : 2 + rows].astype(jnp.float32).reshape(rows * groups, wide)
            added = kept + matmul(taps_of(middle, middle_edge, rows), 4 + 2 * block)
            if block + 1 < blocks:
                settle(current, current_edge, added, rows)
        deliver[tick] = added.reshape(band_rows, groups, wide).astype(jnp.bfloat16)

        @pl.when(tick + 1 < ticks)
        def _():
            latest = reset(deliver[tick].astype(jnp.float32), tick + 1)
            made[tick + 1] = latest.astype(jnp.bfloat16)
            grown[tick + 1, 0, own] = warp(latest, shift_in[tick + 1, 0])
            send_halo(tick + 1, 0)

        @pl.when(tick == 0)
        def _():
            home.start()

        @pl.when(tick > 0)
        def _():
            delivered(tick).start()

        return nothing

    lax.fori_loop(0, ticks, one_tick, 0)

    home.wait()
    for tick in range(ticks):
        for slot in range(3):
            for copy in halo(tick, slot):
                copy.wait_send()
        if tick > 0:
            shifts(tick).wait_send()
            fetched(tick).wait_send()
            delivered(tick).wait_send()
            delivered(tick).wait_recv()


def shards(features, carried, flow_shift, clip_start, join_weight, res_weight):
    ticks, band_rows, line = features.shape
    channels = join_weight.shape[2]
    blocks = res_weight.shape[0] // 2
    row_count = lax.axis_size("rows")
    wide = 2 * LANES
    groups = line // wide
    rim = 1 + 2 * blocks
    most = band_rows + 2 * rim - 2

    def grouped(array):
        return array.reshape(-1, band_rows, groups, wide)

    def vmem(*shape):
        return pltpu.VMEM(shape, jnp.bfloat16)

    whole = pl.BlockSpec(memory_space=pltpu.VMEM)
    scalars = pl.BlockSpec(memory_space=pltpu.SMEM)
    state = (band_rows, groups, wide)
    dma = pltpu.SemaphoreType.DMA
    result = pl.pallas_call(
        functools.partial(kernel, ticks, blocks, row_count),
        out_shape=jax.ShapeDtypeStruct((ticks, *state), jnp.bfloat16),
        in_specs=[whole, whole, scalars, scalars, whole, whole],
        out_specs=pl.BlockSpec(memory_space=pl.ANY),
        scratch_shapes=[
            vmem((3 + 2 * blocks) * 18 * channels, wide),
            vmem(ticks, 3, band_rows + 2 * rim, groups, wide),
            vmem(3, band_rows + 2 * rim, groups, LANES),
            vmem(most, groups, wide),
            vmem(most, groups, LANES),
            vmem(most, groups, wide),
            vmem(most, groups, LANES),
            pltpu.VMEM((most * groups, wide), jnp.float32),
            vmem(ticks, *state),
            vmem(ticks, *state),
            pltpu.VMEM((ticks, 2, groups, LANES), jnp.int32),
            pltpu.VMEM((ticks, 2, groups, LANES), jnp.int32),
            dma((ticks, 3, 2)),
            dma((ticks, 3, 2)),
            dma((ticks,)),
            dma((ticks,)),
            dma((ticks,)),
            dma((ticks,)),
            dma((ticks,)),
            dma((ticks,)),
            dma,
        ],
        compiler_params=pltpu.CompilerParams(
            collective_id=0, has_side_effects=True, vmem_limit_bytes=48 * 1024 * 1024
        ),
    )(grouped(features), grouped(carried), flow_shift.transpose(1, 2, 0), clip_start, join_weight, res_weight)
    return result.reshape(ticks, band_rows, line)


def solution(mesh):
    in_specs = (
        P(None, ("groups", "rows"), None),
        P(None, ("groups", "rows"), None),
        P(None, ("groups", "rows"), None),
        P("groups"),
        P(),
        P(),
    )
    out_specs = P(None, ("groups", "rows"), None)
    return jax.shard_map(shards, mesh=mesh, in_specs=in_specs, out_specs=out_specs, check_vma=False)
```

```python
import functools

import jax
import jax.numpy as jnp
from jax import lax
from jax.experimental import pallas as pl
from jax.experimental.pallas import tpu as pltpu
from jax.sharding import PartitionSpec as P

SECTIONS = 4
MAXSHIFT = 8
LANES = 128


def band_blocks(taps):
    zero = jnp.zeros_like(taps[0])
    blank = jnp.concatenate([zero, zero], axis=1)
    first = jnp.concatenate([taps[0], zero], axis=1)
    second = jnp.concatenate([taps[1], taps[0]], axis=1)
    third = jnp.concatenate([taps[2], taps[1]], axis=1)
    fourth = jnp.concatenate([zero, taps[2]], axis=1)
    return [
        (second, blank),
        (third, first),
        (fourth, second),
        (blank, third),
        (blank, fourth),
        (first, blank),
    ]


def turn(values, step):
    return pltpu.roll(values, step % values.shape[1], axis=1)


def warp(state, shift):
    groups = state.shape[1]
    low, high = state[..., :LANES], state[..., LANES:]
    lane = lax.broadcasted_iota(jnp.int32, (1, groups, LANES), 2)
    group = lax.broadcasted_iota(jnp.int32, (1, groups, LANES), 1)
    left_half = lane < LANES // 2
    shift = shift[None]
    quads = lax.shift_right_arithmetic(shift, 2)
    for mask, step in ((quads < 0, -4), ((quads & 2) != 0, 2), ((quads & 1) != 0, 1)):
        low = jnp.where(mask, turn(low, step), low)
        high = jnp.where(mask, turn(high, step), high)
    two = (shift & 2) != 0
    low, high = jnp.where(two, turn(high, 1), low), jnp.where(two, low, high)
    one = (shift & 1) != 0
    low_swap = pltpu.roll(low, LANES // 2, axis=2)
    high_swap = pltpu.roll(high, LANES // 2, axis=2)
    low = jnp.where(one, jnp.where(left_half, turn(high_swap, 1), low_swap), low)
    high = jnp.where(one, jnp.where(left_half, low_swap, high_swap), high)
    origin = group * 4 + lane // (LANES // 2) - shift
    low = jnp.where((origin >= 0) & (origin < 4 * groups), low, 0.0)
    high = jnp.where((origin >= -2) & (origin < 4 * groups - 2), high, 0.0)
    return jnp.concatenate([low, high], axis=-1).astype(jnp.bfloat16)


def edges(values):
    groups = values.shape[1]
    group = lax.broadcasted_iota(jnp.int32, (1, groups, LANES), 1)
    lane = lax.broadcasted_iota(jnp.int32, (1, groups, LANES), 2)
    left_half = lane < LANES // 2
    edge = jnp.where(left_half, turn(values[..., :LANES], -1), turn(values[..., LANES:], 1))
    outside = (left_half & (group == groups - 1)) | ((lane >= LANES // 2) & (group == 0))
    return jnp.where(outside, 0.0, edge).astype(jnp.bfloat16)


def lay_taps(left, values, start):
    rows = values.shape[0] - 2
    main = values.astype(jnp.bfloat16)
    edge = edges(values)
    for a in range(3):
        column = start + a * 2 * LANES
        left[0:rows, :, column : column + 2 * LANES] = main[a : a + rows]
    for a in range(3):
        column = start + (6 + a) * LANES
        left[0:rows, :, column : column + LANES] = edge[a : a + rows]


def kernel(
    ticks, blocks, row_count, feat, carried, flow, clip, join_w, res_w, out,
    band_w, grown, joined, current, middle, made,
    deliver, shift_out, shift_in,
    halo_send, halo_recv, feat_send, feat_recv, flow_send, flow_recv, out_send, out_recv, local_sem,
):
    band_rows, groups, wide = feat.shape[1:]
    channels = join_w.shape[2]
    rim = 1 + 2 * blocks
    own = pl.ds(rim, band_rows)
    band_count = row_count // SECTIONS
    me = lax.axis_index("rows")
    spot = lax.rem(me - band_count // 2 + row_count, row_count)
    band = lax.rem(spot, band_count)
    owner = lax.div(spot, band_count)

    def at(offset):
        return {"rows": lax.rem(me + offset, row_count)}

    offsets = {1, row_count - 1}
    for tick in range(1, ticks):
        offsets |= {(band_count * tick) % row_count, (-band_count * tick) % row_count}
    barrier = pltpu.get_barrier_semaphore()
    for offset in sorted(offsets):
        pl.semaphore_signal(
            barrier, inc=1, device_id=at(offset), device_id_type=pl.DeviceIdType.MESH
        )

    def copy_of(source, target, send_sem, recv_sem, offset):
        return pltpu.make_async_remote_copy(
            src_ref=source, dst_ref=target, send_sem=send_sem, recv_sem=recv_sem,
            device_id=at(offset), device_id_type=pl.DeviceIdType.MESH,
        )

    def halo(tick, slot):
        block = grown.at[tick, slot]
        return (
            copy_of(block.at[pl.ds(band_rows, rim)], block.at[pl.ds(0, rim)],
                    halo_send.at[tick, slot, 0], halo_recv.at[tick, slot, 0], 1),
            copy_of(block.at[pl.ds(rim, rim)], block.at[pl.ds(rim + band_rows, rim)],
                    halo_send.at[tick, slot, 1], halo_recv.at[tick, slot, 1], row_count - 1),
        )

    def send_halo(tick, slot):
        for copy in halo(tick, slot):
            copy.start()

    def backwards(tick):
        return row_count - band_count * tick

    def fetched(tick):
        return copy_of(feat.at[tick], grown.at[tick, 2, own], feat_send.at[tick],
                       feat_recv.at[tick], backwards(tick))

    def shifts(tick):
        return copy_of(shift_out.at[tick], shift_in.at[tick], flow_send.at[tick],
                       flow_recv.at[tick], backwards(tick))

    def delivered(tick):
        return copy_of(deliver.at[tick], out.at[tick], out_send.at[tick], out_recv.at[tick],
                       band_count * tick)

    home = pltpu.make_async_copy(deliver.at[0], out.at[0], local_sem)

    def reset(state, tick):
        begins = clip[lax.rem(owner + tick, SECTIONS)]
        keep = jnp.full((groups, wide), begins, jnp.int32) != tick
        return jnp.where(keep[None], state, 0.0)

    grown[0, 2, own] = feat[0]
    for tick in range(1, ticks):
        for which in range(2):
            shift_out[tick, which] = jnp.full((groups, LANES), flow[0, which, tick], jnp.int32)
    pl.semaphore_wait(barrier, len(offsets))
    send_halo(0, 2)
    for slot in (1, 0):
        state = reset(carried[slot].astype(jnp.float32), 0)
        if slot == 0:
            made[0] = state.astype(jnp.bfloat16)
        shift = jnp.full((groups, LANES), flow[0, slot, 0], jnp.int32)
        grown[0, slot, own] = warp(state, shift)
        send_halo(0, slot)
    for tick in range(1, ticks):
        shifts(tick).start()

    depth = 18 * channels
    for layer in range(3 + 2 * blocks):
        base = layer * depth
        for kernel_row in range(3):
            taps = []
            for column in range(3):
                if layer < 3:
                    start = (column * 3 + layer) * channels
                    taps.append(join_w[kernel_row, start : start + channels, :])
                else:
                    start = column * channels
                    taps.append(res_w[layer - 3, kernel_row, start : start + channels, :])
            for index, (left_part, right_part) in enumerate(band_blocks(taps)):
                if index < 4:
                    start = (kernel_row * 4 + index) * channels
                else:
                    start = (12 + kernel_row * 2 + index - 4) * channels
                band_w[base + start : base + start + channels, 0:LANES] = left_part
                band_w[base + start : base + start + channels, LANES : 2 * LANES] = right_part

    if ticks > 1:
        fetched(1).start()

    def matmul(left, layer, rows, slots=1, start=0):
        return jnp.dot(
            left[0:rows, :, start : start + slots * depth].reshape(rows * groups, slots * depth),
            band_w[layer * depth : (layer + slots) * depth],
            preferred_element_type=jnp.float32,
        ).reshape(rows, groups, wide)

    def framed(values, margin):
        rows = values.shape[0]
        top = jnp.where(band > 0, values[:margin], 0.0)
        bottom = jnp.where(band < band_count - 1, values[rows - margin :], 0.0)
        return jnp.concatenate([top, values[margin : rows - margin], bottom], axis=0)

    def settle(left, values):
        rounded = values.astype(jnp.bfloat16).astype(jnp.float32)
        lay_taps(left, framed(rounded, (values.shape[0] - band_rows) // 2), 0)

    most = band_rows + 2 * rim - 2

    def lay_join(tick, slot):
        for copy in halo(tick, slot):
            copy.wait_recv()
        lay_taps(joined, framed(grown[tick, slot].astype(jnp.float32), rim), slot * depth)

    def one_tick(tick, nothing):
        lay_join(tick, 1)
        lay_join(tick, 2)
        side = matmul(joined, 1, most, 2, depth)
        lay_join(tick, 0)
        summed = side + matmul(joined, 0, most)
        settle(current, jnp.where(summed >= 0, summed, 0.1 * summed))
        rows = most
        for block in range(blocks):
            rows -= 2
            settle(middle, jnp.maximum(matmul(current, 3 + 2 * block, rows), 0.0))
            if block == 0:
                @pl.when(tick + 1 < ticks)
                def _():
                    shifts(tick + 1).wait_recv()
                    earlier = reset(made[tick].astype(jnp.float32), tick + 1)
                    grown[tick + 1, 1, own] = warp(earlier, shift_in[tick + 1, 1])
                    send_halo(tick + 1, 1)
            if block == blocks - 1:
                @pl.when(tick + 1 < ticks)
                def _():
                    fetched(tick + 1).wait_recv()
                    send_halo(tick + 1, 2)

                @pl.when(tick + 2 < ticks)
                def _():
                    fetched(tick + 2).start()
            rows -= 2
            kept = current[1 : 1 + rows, :, wide : 2 * wide].astype(jnp.float32)
            added = kept + matmul(middle, 4 + 2 * block, rows)
            if block + 1 < blocks:
                settle(current, added)
        deliver[tick] = added.astype(jnp.bfloat16)

        @pl.when(tick + 1 < ticks)
        def _():
            latest = reset(deliver[tick].astype(jnp.float32), tick + 1)
            made[tick + 1] = latest.astype(jnp.bfloat16)
            grown[tick + 1, 0, own] = warp(latest, shift_in[tick + 1, 0])
            send_halo(tick + 1, 0)

        @pl.when(tick == 0)
        def _():
            home.start()

        @pl.when(tick > 0)
        def _():
            delivered(tick).start()

        return nothing

    lax.fori_loop(0, ticks, one_tick, 0)

    home.wait()
    for tick in range(ticks):
        for slot in range(3):
            for copy in halo(tick, slot):
                copy.wait_send()
        if tick > 0:
            shifts(tick).wait_send()
            fetched(tick).wait_send()
            delivered(tick).wait_send()
            delivered(tick).wait_recv()


def shards(features, carried, flow_shift, clip_start, join_weight, res_weight):
    ticks, band_rows, line = features.shape
    channels = join_weight.shape[2]
    blocks = res_weight.shape[0] // 2
    row_count = lax.axis_size("rows")
    wide = 2 * LANES
    groups = line // wide
    rim = 1 + 2 * blocks
    most = band_rows + 2 * rim - 2

    def grouped(array):
        return array.reshape(-1, band_rows, groups, wide)

    def vmem(*shape):
        return pltpu.VMEM(shape, jnp.bfloat16)

    whole = pl.BlockSpec(memory_space=pltpu.VMEM)
    scalars = pl.BlockSpec(memory_space=pltpu.SMEM)
    state = (band_rows, groups, wide)
    dma = pltpu.SemaphoreType.DMA
    result = pl.pallas_call(
        functools.partial(kernel, ticks, blocks, row_count),
        out_shape=jax.ShapeDtypeStruct((ticks, *state), jnp.bfloat16),
        in_specs=[whole, whole, scalars, scalars, whole, whole],
        out_specs=pl.BlockSpec(memory_space=pl.ANY),
        scratch_shapes=[
            vmem((3 + 2 * blocks) * 18 * channels, wide),
            vmem(ticks, 3, band_rows + 2 * rim, groups, wide),
            vmem(most, groups, 27 * LANES),
            vmem(most - 2, groups, 9 * LANES),
            vmem(most - 4, groups, 9 * LANES),
            vmem(ticks, *state),
            vmem(ticks, *state),
            pltpu.VMEM((ticks, 2, groups, LANES), jnp.int32),
            pltpu.VMEM((ticks, 2, groups, LANES), jnp.int32),
            dma((ticks, 3, 2)),
            dma((ticks, 3, 2)),
            dma((ticks,)),
            dma((ticks,)),
            dma((ticks,)),
            dma((ticks,)),
            dma((ticks,)),
            dma((ticks,)),
            dma,
        ],
        compiler_params=pltpu.CompilerParams(
            collective_id=0, has_side_effects=True, vmem_limit_bytes=48 * 1024 * 1024
        ),
    )(grouped(features), grouped(carried), flow_shift.transpose(1, 2, 0), clip_start, join_weight, res_weight)
    return result.reshape(ticks, band_rows, line)


def solution(mesh):
    in_specs = (
        P(None, ("groups", "rows"), None),
        P(None, ("groups", "rows"), None),
        P(None, ("groups", "rows"), None),
        P("groups"),
        P(),
        P(),
    )
    out_specs = P(None, ("groups", "rows"), None)
    return jax.shard_map(shards, mesh=mesh, in_specs=in_specs, out_specs=out_specs, check_vma=False)
```

```python
import functools

import jax
import jax.numpy as jnp
from jax import lax
from jax.experimental import pallas as pl
from jax.experimental.pallas import tpu as pltpu
from jax.sharding import PartitionSpec as P

SECTIONS = 4
PIECES = 4
LANES = 128


def band_blocks(taps):
    zero = jnp.zeros_like(taps[0])
    blank = jnp.concatenate([zero, zero], axis=1)
    first = jnp.concatenate([taps[0], zero], axis=1)
    second = jnp.concatenate([taps[1], taps[0]], axis=1)
    third = jnp.concatenate([taps[2], taps[1]], axis=1)
    fourth = jnp.concatenate([zero, taps[2]], axis=1)
    return [
        (second, blank),
        (third, first),
        (fourth, second),
        (blank, third),
        (blank, fourth),
        (first, blank),
    ]


def turn(values, step):
    return pltpu.roll(values, step % values.shape[1], axis=1)


def warp(state, shift):
    groups = state.shape[1]
    low, high = state[..., :LANES], state[..., LANES:]
    lane = lax.broadcasted_iota(jnp.int32, (1, groups, LANES), 2)
    group = lax.broadcasted_iota(jnp.int32, (1, groups, LANES), 1)
    left_half = lane < LANES // 2
    shift = shift[None]
    quads = lax.shift_right_arithmetic(shift, 2)
    for mask, step in ((quads < 0, -4), ((quads & 2) != 0, 2), ((quads & 1) != 0, 1)):
        low = jnp.where(mask, turn(low, step), low)
        high = jnp.where(mask, turn(high, step), high)
    two = (shift & 2) != 0
    low, high = jnp.where(two, turn(high, 1), low), jnp.where(two, low, high)
    one = (shift & 1) != 0
    low_swap = pltpu.roll(low, LANES // 2, axis=2)
    high_swap = pltpu.roll(high, LANES // 2, axis=2)
    low = jnp.where(one, jnp.where(left_half, turn(high_swap, 1), low_swap), low)
    high = jnp.where(one, jnp.where(left_half, low_swap, high_swap), high)
    origin = group * 4 + lane // (LANES // 2) - shift
    low = jnp.where((origin >= 0) & (origin < 4 * groups), low, 0.0)
    high = jnp.where((origin >= -2) & (origin < 4 * groups - 2), high, 0.0)
    return jnp.concatenate([low, high], axis=-1).astype(jnp.bfloat16)


def edges(values):
    groups = values.shape[1]
    group = lax.broadcasted_iota(jnp.int32, (1, groups, LANES), 1)
    lane = lax.broadcasted_iota(jnp.int32, (1, groups, LANES), 2)
    left_half = lane < LANES // 2
    edge = jnp.where(left_half, turn(values[..., :LANES], -1), turn(values[..., LANES:], 1))
    outside = (left_half & (group == groups - 1)) | ((lane >= LANES // 2) & (group == 0))
    return jnp.where(outside, 0.0, edge).astype(jnp.bfloat16)


def lay_taps(left, values, start):
    rows = values.shape[0] - 2
    main = values.astype(jnp.bfloat16)
    edge = edges(values)
    for a in range(3):
        column = start + a * 2 * LANES
        left[0:rows, :, column : column + 2 * LANES] = main[a : a + rows]
    for a in range(3):
        column = start + (6 + a) * LANES
        left[0:rows, :, column : column + LANES] = edge[a : a + rows]


def kernel(
    ticks, blocks, row_count, feat, carried, flow, clip, join_w, res_w, out,
    band_w, grown, joined, current, middle, made,
    deliver, shift_out, shift_in,
    halo_send, halo_recv, feat_send, feat_recv, flow_send, flow_recv, out_send, out_recv, local_sem,
):
    band_rows, groups, wide = feat.shape[1:]
    channels = join_w.shape[2]
    rim = 1 + 2 * blocks
    own = pl.ds(rim, band_rows)
    band_count = row_count // SECTIONS
    me = lax.axis_index("rows")
    spot = lax.rem(me - band_count // 2 + row_count, row_count)
    band = lax.rem(spot, band_count)
    owner = lax.div(spot, band_count)

    def at(offset):
        return {"rows": lax.rem(me + offset, row_count)}

    offsets = {1, row_count - 1}
    for tick in range(1, ticks):
        offsets |= {(band_count * tick) % row_count, (-band_count * tick) % row_count}
    barrier = pltpu.get_barrier_semaphore()
    for offset in sorted(offsets):
        pl.semaphore_signal(
            barrier, inc=1, device_id=at(offset), device_id_type=pl.DeviceIdType.MESH
        )

    def copy_of(source, target, send_sem, recv_sem, offset):
        return pltpu.make_async_remote_copy(
            src_ref=source, dst_ref=target, send_sem=send_sem, recv_sem=recv_sem,
            device_id=at(offset), device_id_type=pl.DeviceIdType.MESH,
        )

    def halo(tick, slot):
        block = grown.at[tick, slot]
        return (
            copy_of(block.at[pl.ds(band_rows, rim)], block.at[pl.ds(0, rim)],
                    halo_send.at[tick, slot, 0], halo_recv.at[tick, slot, 0], 1),
            copy_of(block.at[pl.ds(rim, rim)], block.at[pl.ds(rim + band_rows, rim)],
                    halo_send.at[tick, slot, 1], halo_recv.at[tick, slot, 1], row_count - 1),
        )

    def send_halo(tick, slot):
        down, up = halo(tick, slot)
        pl.when(band < band_count - 1)(down.start)
        pl.when(band > 0)(up.start)

    def await_halo(tick, slot):
        from_above, from_below = halo(tick, slot)
        pl.when(band > 0)(from_above.wait_recv)
        pl.when(band < band_count - 1)(from_below.wait_recv)

    def finish_halo(tick, slot):
        down, up = halo(tick, slot)
        pl.when(band < band_count - 1)(down.wait_send)
        pl.when(band > 0)(up.wait_send)

    def backwards(tick):
        return row_count - band_count * tick

    piece = band_rows // PIECES

    def fetched(tick):
        return [
            copy_of(feat.at[tick, pl.ds(part * piece, piece)],
                    grown.at[tick, 2, pl.ds(rim + part * piece, piece)],
                    feat_send.at[tick, part], feat_recv.at[tick, part], backwards(tick))
            for part in range(PIECES)
        ]

    def fetch(tick):
        for copy in fetched(tick):
            copy.start()

    def shifts(tick):
        return copy_of(shift_out.at[tick], shift_in.at[tick], flow_send.at[tick],
                       flow_recv.at[tick], backwards(tick))

    def delivered(tick):
        return [
            copy_of(deliver.at[tick, pl.ds(part * piece, piece)],
                    out.at[tick, pl.ds(part * piece, piece)],
                    out_send.at[tick, part], out_recv.at[tick, part], band_count * tick)
            for part in range(PIECES)
        ]

    home = pltpu.make_async_copy(deliver.at[0], out.at[0], local_sem)

    def reset(state, tick):
        begins = clip[lax.rem(owner + tick, SECTIONS)]
        keep = jnp.full((groups, wide), begins, jnp.int32) != tick
        return jnp.where(keep[None], state, 0.0)

    grown[0, 2, own] = feat[0]
    for tick in range(1, ticks):
        for which in range(2):
            shift_out[tick, which] = jnp.full((groups, LANES), flow[0, which, tick], jnp.int32)
    pl.semaphore_wait(barrier, len(offsets))
    send_halo(0, 2)
    for slot in (1, 0):
        state = reset(carried[slot].astype(jnp.float32), 0)
        if slot == 0:
            made[0] = state.astype(jnp.bfloat16)
        shift = jnp.full((groups, LANES), flow[0, slot, 0], jnp.int32)
        grown[0, slot, own] = warp(state, shift)
        send_halo(0, slot)
    for tick in range(1, ticks):
        shifts(tick).start()

    depth = 18 * channels
    for layer in range(3 + 2 * blocks):
        base = layer * depth
        for kernel_row in range(3):
            taps = []
            for column in range(3):
                if layer < 3:
                    start = (column * 3 + layer) * channels
                    taps.append(join_w[kernel_row, start : start + channels, :])
                else:
                    start = column * channels
                    taps.append(res_w[layer - 3, kernel_row, start : start + channels, :])
            for index, (left_part, right_part) in enumerate(band_blocks(taps)):
                if index < 4:
                    start = (kernel_row * 4 + index) * channels
                else:
                    start = (12 + kernel_row * 2 + index - 4) * channels
                band_w[base + start : base + start + channels, 0:LANES] = left_part
                band_w[base + start : base + start + channels, LANES : 2 * LANES] = right_part

    def matmul(left, layer, rows, slots=1, start=0):
        return jnp.dot(
            left[0:rows, :, start : start + slots * depth].reshape(rows * groups, slots * depth),
            band_w[layer * depth : (layer + slots) * depth],
            preferred_element_type=jnp.float32,
        ).reshape(rows, groups, wide)

    def framed(values, margin):
        rows = values.shape[0]
        top = jnp.where(band > 0, values[:margin], 0.0)
        bottom = jnp.where(band < band_count - 1, values[rows - margin :], 0.0)
        return jnp.concatenate([top, values[margin : rows - margin], bottom], axis=0)

    def settle(left, values):
        rounded = values.astype(jnp.bfloat16).astype(jnp.float32)
        lay_taps(left, framed(rounded, (values.shape[0] - band_rows) // 2), 0)

    most = band_rows + 2 * rim - 2

    def lay_join(tick, slot):
        await_halo(tick, slot)
        lay_taps(joined, framed(grown[tick, slot].astype(jnp.float32), rim), slot * depth)

    def one_tick(tick, nothing):
        lay_join(tick, 1)
        lay_join(tick, 2)
        side = matmul(joined, 1, most, 2, depth)
        lay_join(tick, 0)
        if ticks > 1:
            pl.when(tick == 0)(lambda: fetch(1))
        summed = side + matmul(joined, 0, most)
        settle(current, jnp.where(summed >= 0, summed, 0.1 * summed))
        rows = most
        for block in range(blocks):
            rows -= 2
            settle(middle, jnp.maximum(matmul(current, 3 + 2 * block, rows), 0.0))
            if block == 0:
                @pl.when(tick + 1 < ticks)
                def _():
                    shifts(tick + 1).wait_recv()
                    earlier = reset(made[tick].astype(jnp.float32), tick + 1)
                    grown[tick + 1, 1, own] = warp(earlier, shift_in[tick + 1, 1])
                    send_halo(tick + 1, 1)

                @pl.when(tick + 2 < ticks)
                def _():
                    fetch(tick + 2)
            if block == blocks - 1:
                @pl.when(tick + 1 < ticks)
                def _():
                    for copy in fetched(tick + 1):
                        copy.wait_recv()
                    send_halo(tick + 1, 2)
            rows -= 2
            kept = current[1 : 1 + rows, :, wide : 2 * wide].astype(jnp.float32)
            added = kept + matmul(middle, 4 + 2 * block, rows)
            if block + 1 < blocks:
                settle(current, added)
        deliver[tick] = added.astype(jnp.bfloat16)

        @pl.when(tick + 1 < ticks)
        def _():
            latest = reset(deliver[tick].astype(jnp.float32), tick + 1)
            made[tick + 1] = latest.astype(jnp.bfloat16)
            grown[tick + 1, 0, own] = warp(latest, shift_in[tick + 1, 0])
            send_halo(tick + 1, 0)

        @pl.when(tick == 0)
        def _():
            home.start()

        @pl.when(tick > 0)
        def _():
            for copy in delivered(tick):
                copy.start()

        return nothing

    lax.fori_loop(0, ticks, one_tick, 0)

    home.wait()
    for tick in range(ticks):
        for slot in range(3):
            finish_halo(tick, slot)
        if tick > 0:
            shifts(tick).wait_send()
            for copy in fetched(tick):
                copy.wait_send()
            for copy in delivered(tick):
                copy.wait_send()
                copy.wait_recv()


def shards(features, carried, flow_shift, clip_start, join_weight, res_weight):
    ticks, band_rows, line = features.shape
    channels = join_weight.shape[2]
    blocks = res_weight.shape[0] // 2
    row_count = lax.axis_size("rows")
    wide = 2 * LANES
    groups = line // wide
    rim = 1 + 2 * blocks
    most = band_rows + 2 * rim - 2

    def grouped(array):
        return array.reshape(-1, band_rows, groups, wide)

    def vmem(*shape):
        return pltpu.VMEM(shape, jnp.bfloat16)

    whole = pl.BlockSpec(memory_space=pltpu.VMEM)
    scalars = pl.BlockSpec(memory_space=pltpu.SMEM)
    state = (band_rows, groups, wide)
    dma = pltpu.SemaphoreType.DMA
    result = pl.pallas_call(
        functools.partial(kernel, ticks, blocks, row_count),
        out_shape=jax.ShapeDtypeStruct((ticks, *state), jnp.bfloat16),
        in_specs=[whole, whole, scalars, scalars, whole, whole],
        out_specs=pl.BlockSpec(memory_space=pl.ANY),
        scratch_shapes=[
            vmem((3 + 2 * blocks) * 18 * channels, wide),
            vmem(ticks, 3, band_rows + 2 * rim, groups, wide),
            vmem(most, groups, 27 * LANES),
            vmem(most - 2, groups, 9 * LANES),
            vmem(most - 4, groups, 9 * LANES),
            vmem(ticks, *state),
            vmem(ticks, *state),
            pltpu.VMEM((ticks, 2, groups, LANES), jnp.int32),
            pltpu.VMEM((ticks, 2, groups, LANES), jnp.int32),
            dma((ticks, 3, 2)),
            dma((ticks, 3, 2)),
            dma((ticks, PIECES)),
            dma((ticks, PIECES)),
            dma((ticks,)),
            dma((ticks,)),
            dma((ticks, PIECES)),
            dma((ticks, PIECES)),
            dma,
        ],
        compiler_params=pltpu.CompilerParams(
            collective_id=0, has_side_effects=True, vmem_limit_bytes=48 * 1024 * 1024
        ),
    )(grouped(features), grouped(carried), flow_shift.transpose(1, 2, 0), clip_start, join_weight, res_weight)
    return result.reshape(ticks, band_rows, line)


def solution(mesh):
    in_specs = (
        P(None, ("groups", "rows"), None),
        P(None, ("groups", "rows"), None),
        P(None, ("groups", "rows"), None),
        P("groups"),
        P(),
        P(),
    )
    out_specs = P(None, ("groups", "rows"), None)
    return jax.shard_map(shards, mesh=mesh, in_specs=in_specs, out_specs=out_specs, check_vma=False)
```

```python
import functools

import jax
import jax.numpy as jnp
from jax import lax
from jax.experimental import pallas as pl
from jax.experimental.pallas import tpu as pltpu
from jax.sharding import PartitionSpec as P

SECTIONS = 4
PIECES = 4
LANES = 128


def band_blocks(taps):
    zero = jnp.zeros_like(taps[0])
    blank = jnp.concatenate([zero, zero], axis=1)
    first = jnp.concatenate([taps[0], zero], axis=1)
    second = jnp.concatenate([taps[1], taps[0]], axis=1)
    third = jnp.concatenate([taps[2], taps[1]], axis=1)
    fourth = jnp.concatenate([zero, taps[2]], axis=1)
    return [
        (second, blank),
        (third, first),
        (fourth, second),
        (blank, third),
        (blank, fourth),
        (first, blank),
    ]


def turn(values, step):
    return pltpu.roll(values, step % values.shape[1], axis=1)


def warp(state, shift):
    groups = state.shape[1]
    low, high = state[..., :LANES], state[..., LANES:]
    lane = lax.broadcasted_iota(jnp.int32, (1, groups, LANES), 2)
    group = lax.broadcasted_iota(jnp.int32, (1, groups, LANES), 1)
    left_half = lane < LANES // 2
    shift = shift[None]
    quads = lax.shift_right_arithmetic(shift, 2)
    for mask, step in ((quads < 0, -4), ((quads & 2) != 0, 2), ((quads & 1) != 0, 1)):
        low = jnp.where(mask, turn(low, step), low)
        high = jnp.where(mask, turn(high, step), high)
    two = (shift & 2) != 0
    low, high = jnp.where(two, turn(high, 1), low), jnp.where(two, low, high)
    one = (shift & 1) != 0
    low_swap = pltpu.roll(low, LANES // 2, axis=2)
    high_swap = pltpu.roll(high, LANES // 2, axis=2)
    low = jnp.where(one, jnp.where(left_half, turn(high_swap, 1), low_swap), low)
    high = jnp.where(one, jnp.where(left_half, low_swap, high_swap), high)
    origin = group * 4 + lane // (LANES // 2) - shift
    low = jnp.where((origin >= 0) & (origin < 4 * groups), low, 0.0)
    high = jnp.where((origin >= -2) & (origin < 4 * groups - 2), high, 0.0)
    return jnp.concatenate([low, high], axis=-1).astype(jnp.bfloat16)


def edges(values):
    groups = values.shape[1]
    group = lax.broadcasted_iota(jnp.int32, (1, groups, LANES), 1)
    lane = lax.broadcasted_iota(jnp.int32, (1, groups, LANES), 2)
    left_half = lane < LANES // 2
    edge = jnp.where(left_half, turn(values[..., :LANES], -1), turn(values[..., LANES:], 1))
    outside = (left_half & (group == groups - 1)) | ((lane >= LANES // 2) & (group == 0))
    return jnp.where(outside, 0.0, edge).astype(jnp.bfloat16)


def lay_taps(left, values, start):
    rows = values.shape[0] - 2
    main = values.astype(jnp.bfloat16)
    edge = edges(values)
    for a in range(3):
        column = start + a * 2 * LANES
        left[0:rows, :, column : column + 2 * LANES] = main[a : a + rows]
    for a in range(3):
        column = start + (6 + a) * LANES
        left[0:rows, :, column : column + LANES] = edge[a : a + rows]


def kernel(
    ticks, blocks, row_count, feat, carried, flow, clip, join_stored, res_stored, out,
    join_w, res_w, band_w, grown, joined, current, middle, made,
    deliver, shift_out, shift_in,
    halo_send, halo_recv, feat_send, feat_recv, flow_send, flow_recv, out_send, out_recv, local_sem, join_sem, res_sem,
):
    band_rows, groups, wide = feat.shape[1:]
    channels = join_w.shape[1]
    rim = 1 + 2 * blocks
    own = pl.ds(rim, band_rows)
    band_count = row_count // SECTIONS
    me = lax.axis_index("rows")
    spot = lax.rem(me - band_count // 2 + row_count, row_count)
    band = lax.rem(spot, band_count)
    owner = lax.div(spot, band_count)

    def at(offset):
        return {"rows": lax.rem(me + offset, row_count)}

    offsets = {1, row_count - 1}
    for tick in range(1, ticks):
        offsets |= {(band_count * tick) % row_count, (-band_count * tick) % row_count}
    join_load = pltpu.make_async_copy(join_stored, join_w, join_sem)
    res_load = pltpu.make_async_copy(res_stored, res_w, res_sem)
    join_load.start()
    res_load.start()
    barrier = pltpu.get_barrier_semaphore()
    for offset in sorted(offsets):
        pl.semaphore_signal(
            barrier, inc=1, device_id=at(offset), device_id_type=pl.DeviceIdType.MESH
        )

    def copy_of(source, target, send_sem, recv_sem, offset):
        return pltpu.make_async_remote_copy(
            src_ref=source, dst_ref=target, send_sem=send_sem, recv_sem=recv_sem,
            device_id=at(offset), device_id_type=pl.DeviceIdType.MESH,
        )

    def halo(tick, slot):
        block = grown.at[tick, slot]
        return (
            copy_of(block.at[pl.ds(band_rows, rim)], block.at[pl.ds(0, rim)],
                    halo_send.at[tick, slot, 0], halo_recv.at[tick, slot, 0], 1),
            copy_of(block.at[pl.ds(rim, rim)], block.at[pl.ds(rim + band_rows, rim)],
                    halo_send.at[tick, slot, 1], halo_recv.at[tick, slot, 1], row_count - 1),
        )

    def send_halo(tick, slot):
        down, up = halo(tick, slot)
        pl.when(band < band_count - 1)(down.start)
        pl.when(band > 0)(up.start)

    def await_halo(tick, slot):
        from_above, from_below = halo(tick, slot)
        pl.when(band > 0)(from_above.wait_recv)
        pl.when(band < band_count - 1)(from_below.wait_recv)

    def finish_halo(tick, slot):
        down, up = halo(tick, slot)
        pl.when(band < band_count - 1)(down.wait_send)
        pl.when(band > 0)(up.wait_send)

    def backwards(tick):
        return row_count - band_count * tick

    piece = band_rows // PIECES

    def fetched(tick):
        return [
            copy_of(feat.at[tick, pl.ds(part * piece, piece)],
                    grown.at[tick, 2, pl.ds(rim + part * piece, piece)],
                    feat_send.at[tick, part], feat_recv.at[tick, part], backwards(tick))
            for part in range(PIECES)
        ]

    def fetch(tick):
        for copy in fetched(tick):
            copy.start()

    def shifts(tick):
        return copy_of(shift_out.at[tick], shift_in.at[tick], flow_send.at[tick],
                       flow_recv.at[tick], backwards(tick))

    def delivered(tick):
        return [
            copy_of(deliver.at[tick, pl.ds(part * piece, piece)],
                    out.at[tick, pl.ds(part * piece, piece)],
                    out_send.at[tick, part], out_recv.at[tick, part], band_count * tick)
            for part in range(PIECES)
        ]

    home = pltpu.make_async_copy(deliver.at[0], out.at[0], local_sem)

    def reset(state, tick):
        begins = clip[lax.rem(owner + tick, SECTIONS)]
        keep = jnp.full((groups, wide), begins, jnp.int32) != tick
        return jnp.where(keep[None], state, 0.0)

    grown[0, 2, own] = feat[0]
    for tick in range(1, ticks):
        for which in range(2):
            shift_out[tick, which] = jnp.full((groups, LANES), flow[0, which, tick], jnp.int32)
    pl.semaphore_wait(barrier, len(offsets))
    send_halo(0, 2)
    for slot in (1, 0):
        state = reset(carried[slot].astype(jnp.float32), 0)
        if slot == 0:
            made[0] = state.astype(jnp.bfloat16)
        shift = jnp.full((groups, LANES), flow[0, slot, 0], jnp.int32)
        grown[0, slot, own] = warp(state, shift)
        send_halo(0, slot)
    for tick in range(1, ticks):
        shifts(tick).start()

    depth = 18 * channels
    join_load.wait()
    res_load.wait()
    for layer in range(3 + 2 * blocks):
        base = layer * depth
        for kernel_row in range(3):
            if layer < 3:
                stored = [
                    join_w[kernel_row, :, (column * 3 + layer) * channels : (column * 3 + layer + 1) * channels]
                    for column in range(3)
                ]
            else:
                stored = [
                    res_w[layer - 3, kernel_row, :, column * channels : (column + 1) * channels]
                    for column in range(3)
                ]
            taps = [tap.astype(jnp.float32).T.astype(jnp.bfloat16) for tap in stored]
            for index, (left_part, right_part) in enumerate(band_blocks(taps)):
                if index < 4:
                    start = (kernel_row * 4 + index) * channels
                else:
                    start = (12 + kernel_row * 2 + index - 4) * channels
                band_w[base + start : base + start + channels, 0:LANES] = left_part
                band_w[base + start : base + start + channels, LANES : 2 * LANES] = right_part

    def matmul(left, layer, rows, slots=1, start=0):
        return jnp.dot(
            left[0:rows, :, start : start + slots * depth].reshape(rows * groups, slots * depth),
            band_w[layer * depth : (layer + slots) * depth],
            preferred_element_type=jnp.float32,
        ).reshape(rows, groups, wide)

    def framed(values, margin):
        rows = values.shape[0]
        top = jnp.where(band > 0, values[:margin], 0.0)
        bottom = jnp.where(band < band_count - 1, values[rows - margin :], 0.0)
        return jnp.concatenate([top, values[margin : rows - margin], bottom], axis=0)

    def settle(left, values):
        rounded = values.astype(jnp.bfloat16).astype(jnp.float32)
        lay_taps(left, framed(rounded, (values.shape[0] - band_rows) // 2), 0)

    most = band_rows + 2 * rim - 2

    def lay_join(tick, slot):
        await_halo(tick, slot)
        lay_taps(joined, framed(grown[tick, slot].astype(jnp.float32), rim), slot * depth)

    def one_tick(tick, nothing):
        lay_join(tick, 1)
        lay_join(tick, 2)
        side = matmul(joined, 1, most, 2, depth)
        lay_join(tick, 0)
        if ticks > 1:
            pl.when(tick == 0)(lambda: fetch(1))
        summed = side + matmul(joined, 0, most)
        settle(current, jnp.where(summed >= 0, summed, 0.1 * summed))
        rows = most
        for block in range(blocks):
            rows -= 2
            settle(middle, jnp.maximum(matmul(current, 3 + 2 * block, rows), 0.0))
            if block == 0:
                @pl.when(tick + 1 < ticks)
                def _():
                    shifts(tick + 1).wait_recv()
                    earlier = reset(made[tick].astype(jnp.float32), tick + 1)
                    grown[tick + 1, 1, own] = warp(earlier, shift_in[tick + 1, 1])
                    send_halo(tick + 1, 1)

                @pl.when(tick + 2 < ticks)
                def _():
                    fetch(tick + 2)
            if block == blocks - 1:
                @pl.when(tick + 1 < ticks)
                def _():
                    for copy in fetched(tick + 1):
                        copy.wait_recv()
                    send_halo(tick + 1, 2)
            rows -= 2
            kept = current[1 : 1 + rows, :, wide : 2 * wide].astype(jnp.float32)
            added = kept + matmul(middle, 4 + 2 * block, rows)
            if block + 1 < blocks:
                settle(current, added)
        deliver[tick] = added.astype(jnp.bfloat16)

        @pl.when(tick + 1 < ticks)
        def _():
            latest = reset(deliver[tick].astype(jnp.float32), tick + 1)
            made[tick + 1] = latest.astype(jnp.bfloat16)
            grown[tick + 1, 0, own] = warp(latest, shift_in[tick + 1, 0])
            send_halo(tick + 1, 0)

        @pl.when(tick == 0)
        def _():
            home.start()

        @pl.when(tick > 0)
        def _():
            for copy in delivered(tick):
                copy.start()

        return nothing

    lax.fori_loop(0, ticks, one_tick, 0)

    home.wait()
    for tick in range(ticks):
        for slot in range(3):
            finish_halo(tick, slot)
        if tick > 0:
            shifts(tick).wait_send()
            for copy in fetched(tick):
                copy.wait_send()
            for copy in delivered(tick):
                copy.wait_send()
                copy.wait_recv()


def shards(features, carried, flow_shift, clip_start, join_weight, res_weight):
    ticks, band_rows, line = features.shape
    channels = join_weight.shape[2]
    blocks = res_weight.shape[0] // 2
    row_count = lax.axis_size("rows")
    wide = 2 * LANES
    groups = line // wide
    rim = 1 + 2 * blocks
    most = band_rows + 2 * rim - 2

    def grouped(array):
        return array.reshape(-1, band_rows, groups, wide)

    def vmem(*shape):
        return pltpu.VMEM(shape, jnp.bfloat16)

    whole = pl.BlockSpec(memory_space=pltpu.VMEM)
    stored = pl.BlockSpec(memory_space=pl.ANY)
    scalars = pl.BlockSpec(memory_space=pltpu.SMEM)
    state = (band_rows, groups, wide)
    dma = pltpu.SemaphoreType.DMA
    result = pl.pallas_call(
        functools.partial(kernel, ticks, blocks, row_count),
        out_shape=jax.ShapeDtypeStruct((ticks, *state), jnp.bfloat16),
        in_specs=[whole, whole, scalars, scalars, stored, stored],
        out_specs=pl.BlockSpec(memory_space=pl.ANY),
        scratch_shapes=[
            vmem(*join_weight.transpose(0, 2, 1).shape),
            vmem(*res_weight.transpose(0, 1, 3, 2).shape),
            vmem((3 + 2 * blocks) * 18 * channels, wide),
            vmem(ticks, 3, band_rows + 2 * rim, groups, wide),
            vmem(most, groups, 27 * LANES),
            vmem(most - 2, groups, 9 * LANES),
            vmem(most - 4, groups, 9 * LANES),
            vmem(ticks, *state),
            vmem(ticks, *state),
            pltpu.VMEM((ticks, 2, groups, LANES), jnp.int32),
            pltpu.VMEM((ticks, 2, groups, LANES), jnp.int32),
            dma((ticks, 3, 2)),
            dma((ticks, 3, 2)),
            dma((ticks, PIECES)),
            dma((ticks, PIECES)),
            dma((ticks,)),
            dma((ticks,)),
            dma((ticks, PIECES)),
            dma((ticks, PIECES)),
            dma,
            dma,
            dma,
        ],
        compiler_params=pltpu.CompilerParams(
            collective_id=0, has_side_effects=True, vmem_limit_bytes=48 * 1024 * 1024
        ),
    )(
        grouped(features), grouped(carried), flow_shift.transpose(1, 2, 0), clip_start,
        join_weight.transpose(0, 2, 1), res_weight.transpose(0, 1, 3, 2),
    )
    return result.reshape(ticks, band_rows, line)


def solution(mesh):
    in_specs = (
        P(None, ("groups", "rows"), None),
        P(None, ("groups", "rows"), None),
        P(None, ("groups", "rows"), None),
        P("groups"),
        P(),
        P(),
    )
    out_specs = P(None, ("groups", "rows"), None)
    return jax.shard_map(shards, mesh=mesh, in_specs=in_specs, out_specs=out_specs, check_vma=False)
```
